512 devices in a mesh: replica: 32 (over z, y_hi), tensor: 16 (over y_lo, x, core).
Axes of the slice: x: 4, y: 4 (y_hi: 2, y_lo: 2; y = y_hi * 2 + y_lo), z: 16, core: 2. Of those that a mesh axis runs over, the one named last changes fastest.
Arguments:
- key_head_weight: bfloat16 [16, 128, 8192], P('tensor'), may hold values from -6 to 6
- down_factor_slots: float32 [32, 2, 8192], P('replica', None, 'tensor'), may hold values from -6 to 6
- adapter_up_factor: float32 [64, 1024], P('replica'), may hold values from -0.2 to 0.2
- piece_slot_index: int32 [32], replicated, may hold values from 0 to 31, each once
Outputs:
- merged: bfloat16 [16, 128, 8192], P('tensor')
The draws below stay inside these ranges and needn't reach their ends.
Inputs may be any that keep to these rules, and one draw needn't show every extreme that they name: Piece p lies in slot piece_slot_index[p] of down_factor_slots; every slot holds exactly one piece.
All inputs are finite; a program needn't handle non-finite values.
Results may differ from the reference program's by a relative error of at most 0.001.
Values sent between devices are 32-bit elements; how exact they have to be, the bound alone decides.
A program may use at most 64 MiB of HBM per device.

```python
import jax
import jax.numpy as jnp
from jax import lax

D = 8192
KV_HEADS = 8
ADAPTER_RANK = 64
KEY_OUTPUT_UNITS = 1024
UNITS_DEV = 128
PIECES = 32
ROWS = 2
N_TENSOR = 16


def level_of(key, extent, shards, smallest, largest):
    def one(position, parts):
        heights = jax.random.uniform(jax.random.fold_in(jax.random.fold_in(key, 6), position), (parts,), jnp.float32, smallest / len(shards), largest / len(shards))
        return jnp.repeat(jnp.exp(heights), extent[position] // parts).reshape((-1,) + (1,) * (len(extent) - position - 1))

    loudness = one(*shards[0])
    for cut in shards[1:]:
        loudness = loudness * one(*cut)
    return loudness


def noise(rng, dims, spread, reach, shards=(), held_as=jnp.bfloat16):
    drawn = spread * jax.random.normal(rng, dims, jnp.float32)
    if shards:
        drawn = drawn * level_of(rng, dims, shards, -0.22, 0.18)
    return jnp.clip(drawn, -reach, reach).astype(held_as)


def setup_inputs(seed: int = 0) -> dict:
    keys = jax.random.split(jax.random.key(seed), 5)
    key_head_weight = noise(keys[0], (N_TENSOR, UNITS_DEV, D), 1.0, 6.0, ((0, 16),))
    down_factor_slots = noise(keys[1], (PIECES, ROWS, D), 1.0, 6.0, ((0, 32), (2, 16)), jnp.float32)
    adapter_up_factor = noise(keys[2], (ADAPTER_RANK, KEY_OUTPUT_UNITS), 0.03125, 0.2, ((0, 32),), jnp.float32)
    piece_slot_index = jax.random.permutation(keys[3], PIECES).astype(jnp.int32)
    return dict(key_head_weight=key_head_weight, down_factor_slots=down_factor_slots, adapter_up_factor=adapter_up_factor, piece_slot_index=piece_slot_index)


def reference(key_head_weight, down_factor_slots, adapter_up_factor, piece_slot_index):
    ordered = jnp.take(down_factor_slots, piece_slot_index.astype(jnp.int32), axis=0)
    down_factor_rows = ordered.reshape(ADAPTER_RANK, D)
    lowrank_update = jnp.dot(adapter_up_factor.T, down_factor_rows, preferred_element_type=jnp.float32, precision=lax.Precision.HIGHEST)
    output_units = key_head_weight.shape[1]
    copies = max(1, N_TENSOR // KV_HEADS)
    blocks = []
    for index in range(N_TENSOR):
        first_index = (index // copies) * output_units
        blocks.append(lowrank_update[first_index:first_index + output_units])
    picked = jnp.stack(blocks, axis=0)
    return (key_head_weight.astype(jnp.float32) + 2.0 * picked).astype(jnp.bfloat16)
```

```python
import jax
import jax.numpy as jnp
from jax import lax
from jax.experimental import pallas as pl
from jax.experimental.pallas import tpu as pltpu
from jax.sharding import PartitionSpec as P

MESH = pl.DeviceIdType.MESH
MERGE_SCALE = 2.0
NX, NY, NZ = 4, 4, 16
LANES = 128
COLUMNS = 512


def place(x, y, z, core):
    return (z * 2 + y // 2, ((y % 2) * NX + x) * 2 + core)


def block_of(x, y, core):
    return (x * NY + y) * 2 + core


def kernel(index_ref, down_ref, up_ref, weight_ref, out_ref, index, tiles, ups, weight, left,
           weight_sem, small_sem, z_send, z_recv, up_send, up_recv, up_pair_send, up_pair_recv,
           xy_send, xy_recv, core_send):
    replica, tensor = lax.axis_index("replica"), lax.axis_index("tensor")
    z, y_hi = replica // 2, replica % 2
    y, x, core = y_hi * 2 + tensor // 8, (tensor // 2) % NX, tensor % 2
    mine = block_of(x, y, core)
    head = tensor // 2

    z_others = []
    for k in range(8, 0, -1):
        z_others.append(lax.rem(z + k, NZ))
        if k < 8:
            z_others.append(lax.rem(z + NZ - k, NZ))
    plane = [((x + dx) % NX, (y + dy) % NY)
             for dx, dy in [(2, 2), (2, 1), (2, 3), (1, 2), (3, 2), (1, 1), (1, 3), (3, 1), (3, 3),
                            (2, 0), (0, 2), (1, 0), (3, 0), (0, 1), (0, 3)]]

    barrier = pltpu.get_barrier_semaphore()
    for other in z_others:
        pl.semaphore_signal(barrier, inc=1, device_id=place(x, y, other, core), device_id_type=MESH)
    for a, b in plane:
        pl.semaphore_signal(barrier, inc=1, device_id=place(a, b, z, core), device_id_type=MESH)
    pl.semaphore_signal(barrier, inc=1, device_id=place(x, y, z, 1 - core), device_id_type=MESH)

    own_tile = pltpu.make_async_copy(down_ref, tiles.at[mine, z], small_sem.at[0])
    own_up = pltpu.make_async_copy(
        up_ref.at[:, pl.ds(pl.multiple_of(head * LANES, LANES), LANES)], ups.at[y_hi, z], small_sem.at[1])
    get_index = pltpu.make_async_copy(index_ref, index, small_sem.at[2])
    get_weight = pltpu.make_async_copy(weight_ref, weight, weight_sem)
    own_tile.start()
    own_up.start()
    get_index.start()
    get_weight.start()
    own_tile.wait()
    own_up.wait()

    pl.semaphore_wait(barrier, len(z_others) + len(plane) + 1)

    def send(ref, send_sem, recv_sem, where):
        pltpu.make_async_remote_copy(src_ref=ref, dst_ref=ref, send_sem=send_sem, recv_sem=recv_sem,
                                     device_id=where, device_id_type=MESH).start()

    def wait(ref, sem):
        pltpu.make_async_copy(ref, ref, sem).wait()

    for other in z_others:
        send(tiles.at[mine, z], z_send, z_recv, place(x, y, other, core))
    for other in z_others:
        send(ups.at[y_hi, z], up_send, up_recv, place(x, y, other, core))

    wait(tiles.at[mine, pl.ds(0, NZ - 1)], z_recv)
    for a, b in plane:
        send(tiles.at[mine], xy_send, xy_recv.at[mine], place(a, b, z, core))
    send(tiles.at[mine], core_send, xy_recv.at[mine], place(x, y, z, 1 - core))
    wait(ups.at[y_hi, pl.ds(0, NZ - 1)], up_recv)
    send(ups.at[y_hi], up_pair_send, up_pair_recv, place(x, (y + 2) % NY, z, core))

    get_index.wait()
    wait(ups.at[y_hi], up_pair_recv)

    iota = lambda shape, dim: lax.broadcasted_iota(jnp.int32, shape, dim)
    k32 = iota((192, 32), 0) % 64
    slot = (k32 % 16) * 2 + k32 // 32
    holds = (index[...] == slot).astype(jnp.bfloat16)
    q = iota((32, 64), 1)
    spread = (iota((32, 64), 0) == ((q // 2) % 16) * 2 + q // 32).astype(jnp.bfloat16)
    k64, q64 = iota((192, 64), 0), iota((192, 64), 1)
    pick = jnp.dot(holds, spread, preferred_element_type=jnp.float32)
    pick = jnp.where(q64 % 2 == (k64 // 16) % 2, pick, 0.0)
    pick_high = jnp.where(k64 < 128, pick, 0.0).astype(jnp.bfloat16)
    pick_low = jnp.where(k64 < 128, 0.0, pick).astype(jnp.bfloat16)
    rows = MERGE_SCALE * ups[...].reshape(64, LANES)
    turned = rows.T
    high = turned.astype(jnp.bfloat16)
    low = (turned - high.astype(jnp.float32)).astype(jnp.bfloat16)
    nt = (((1,), (1,)), ((), ()))
    left[...] = (lax.dot_general(high, pick_high, nt, preferred_element_type=jnp.float32)
                 + lax.dot_general(low, pick_low, nt, preferred_element_type=jnp.float32)).astype(jnp.bfloat16)
    get_weight.wait()

    def merge(a, b_low, which):
        pair = [block_of(a, b_low, which), block_of(a, b_low + 2, which)]
        parts = []
        for c in range(4):
            parts.append(jnp.concatenate(
                [tiles[w, :, c * 2 + i, :] for w in pair for i in range(2)], axis=0))
        right = jnp.concatenate(parts, axis=1)
        right_high = right.astype(jnp.bfloat16)
        right_low = (right - right_high.astype(jnp.float32)).astype(jnp.bfloat16)
        right = jnp.concatenate([right_high, right_low, right_high], axis=0)
        update = jnp.dot(left[...], right, preferred_element_type=jnp.float32)
        at = pl.ds(pl.multiple_of(((b_low * NX + a) * 2 + which) * COLUMNS, COLUMNS), COLUMNS)
        out_ref[:, at] = (weight[:, at].astype(jnp.float32) + update).astype(jnp.bfloat16)

    def offsets(p):
        q = p // 2
        return q + (q // 2) * (1 - 2 * (q % 2)), p % 2

    def step(p, carry):
        dx, dy = offsets(p)
        a, b, b2 = (x + dx) % NX, (y + dy) % NY, (y + dy + 2) % NY
        first, second = block_of(a, b, core), block_of(a, b2, core)

        @pl.when(p > 0)
        def _():
            wait(tiles.at[first], xy_recv.at[first])
            send(tiles.at[first], core_send, xy_recv.at[first], place(x, y, z, 1 - core))

        wait(tiles.at[second], xy_recv.at[second])
        send(tiles.at[second], core_send, xy_recv.at[second], place(x, y, z, 1 - core))
        merge(a, b % 2, core)

        @pl.when(p > 0)
        def _():
            sibling(p - 1)

        return carry

    def sibling(p):
        dx, dy = offsets(p)
        a, b, b2 = (x + dx) % NX, (y + dy) % NY, (y + dy + 2) % NY
        for w in (block_of(a, b, 1 - core), block_of(a, b2, 1 - core)):
            wait(tiles.at[w], xy_recv.at[w])
        merge(a, b % 2, 1 - core)

    lax.fori_loop(0, 8, step, 0)
    sibling(7)

    wait(tiles.at[mine, pl.ds(0, NZ - 1)], z_send)
    wait(ups.at[y_hi, pl.ds(0, NZ - 1)], up_send)
    wait(ups.at[y_hi], up_pair_send)
    wait(tiles.at[pl.ds(0, 15)], xy_send)
    wait(tiles.at[pl.ds(0, 16)], core_send)


def local(key_head_weight, down_factor_slots, adapter_up_factor, piece_slot_index):
    units, width = key_head_weight.shape[1:]
    tile = down_factor_slots.reshape(2, 4, LANES).transpose(1, 0, 2).reshape(8, LANES)
    dma = pltpu.SemaphoreType.DMA
    merged = pl.pallas_call(
        kernel,
        out_shape=jax.ShapeDtypeStruct((units, width), jnp.bfloat16),
        in_specs=[pl.BlockSpec(memory_space=pltpu.HBM)] * 4,
        out_specs=pl.BlockSpec(memory_space=pltpu.VMEM),
        scratch_shapes=[
            pltpu.VMEM((1, 32), jnp.int32),
            pltpu.VMEM((32, NZ, 8, LANES), jnp.float32),
            pltpu.VMEM((2, NZ, 2, LANES), jnp.float32),
            pltpu.VMEM((units, width), jnp.bfloat16),
            pltpu.VMEM((units, 192), jnp.bfloat16),
            dma, dma((3,)), dma, dma, dma, dma, dma, dma, dma, dma((32,)), dma,
        ],
        compiler_params=pltpu.CompilerParams(
            collective_id=0, has_side_effects=True, vmem_limit_bytes=32 << 20),
        name="gather_and_merge",
    )(piece_slot_index.reshape(1, 32), tile, adapter_up_factor, key_head_weight.reshape(units, width))
    return merged.reshape(1, units, width)


def solution(mesh):
    in_specs = (P("tensor", None, None), P("replica", None, "tensor"), P("replica", None), P())
    out_specs = P("tensor", None, None)
    return jax.shard_map(local, mesh=mesh, in_specs=in_specs, out_specs=out_specs, check_vma=False)
```

```python
import jax
import jax.numpy as jnp
from jax import lax
from jax.experimental import pallas as pl
from jax.experimental.pallas import tpu as pltpu
from jax.sharding import PartitionSpec as P

MESH = pl.DeviceIdType.MESH
MERGE_SCALE = 2.0
NX, NY, NZ = 4, 4, 16
CUBE = 4
HALF = 8
LANES = 128
COLUMNS = 512
PLANE = [(2, 2), (2, 1), (2, 3), (1, 2), (3, 2), (1, 1), (1, 3), (3, 1), (3, 3),
         (2, 0), (0, 2), (1, 0), (3, 0), (0, 1), (0, 3)]


def place(x, y, z, core):
    return (z * 2 + y // 2, ((y % 2) * NX + x) * 2 + core)


def block_of(x, y, core):
    return (core * NX + x) * NY + y


def exchanged(z):
    return z + CUBE * (z // HALF) * (1 - 2 * ((z // CUBE) % 2))


def kernel(index_ref, down_ref, up_ref, weight_ref, out_ref, index, tiles, ups, pair_up, weight, left,
           weight_sem, small_sem, z_send, z_recv, pair_send, pair_recv, up_send, up_recv,
           forward_send, up_forward_send, xy_send, xy_recv, core_send, core_recv):
    replica, tensor = lax.axis_index("replica"), lax.axis_index("tensor")
    z, y_hi = replica // 2, replica % 2
    y, x, core = y_hi * 2 + tensor // 8, (tensor // 2) % NX, tensor % 2
    mine, slot = block_of(x, y, core), exchanged(z)
    first, second = z < CUBE, z // CUBE == 1
    last, not_first = z >= HALF, z >= CUBE

    def column(k):
        return place(x, y, k, core)

    plane = [place((x + dx) % NX, (y + dy) % NY, z, core) for dx, dy in PLANE]
    partner = place(x, y, z, 1 - core)

    barrier = pltpu.get_barrier_semaphore()

    def signal(where):
        pl.semaphore_signal(barrier, inc=1, device_id=where, device_id_type=MESH)

    @pl.when(z < HALF)
    def _():
        for k in range(HALF, NZ):
            signal(column(k))

    @pl.when(first)
    def _():
        for k in range(CUBE, HALF):
            signal(column(k))
        for k in range(1, CUBE):
            signal(column((z + k) % CUBE))

    for where in plane:
        signal(where)
    signal(partner)

    my_up = up_ref.at[:, pl.ds(pl.multiple_of(tensor // 2 * LANES, LANES), LANES)]
    own_tile = pltpu.make_async_copy(down_ref, tiles.at[mine, slot], small_sem.at[0])
    own_up = pltpu.make_async_copy(my_up, pair_up.at[y_hi], small_sem.at[1])
    get_index = pltpu.make_async_copy(index_ref, index, small_sem.at[2])
    get_weight = pltpu.make_async_copy(weight_ref, weight, weight_sem)

    @pl.when(first)
    def _():
        own_tile.start()

    own_up.start()
    get_index.start()
    get_weight.start()

    def copy(source, target, send_sem, recv_sem, where):
        pltpu.make_async_remote_copy(src_ref=source, dst_ref=target, send_sem=send_sem, recv_sem=recv_sem,
                                     device_id=where, device_id_type=MESH).start()

    def send(ref, send_sem, recv_sem, where):
        copy(ref, ref, send_sem, recv_sem, where)

    def wait(ref, sem):
        pltpu.make_async_copy(ref, ref, sem).wait()

    def slots(w, start, size):
        return tiles.at[w, pl.ds(start, size)]

    def over_plane(g, start, size):
        for where in plane:
            send(slots(mine, start, size), xy_send, xy_recv.at[x, g], where)

    def exchange_ups(others):
        copy(my_up, pair_up.at[y_hi], pair_send, pair_recv, place(x, (y + 2) % NY, z, core))
        own_up.wait()
        wait(pair_up.at[1 - y_hi], pair_recv)
        for where in others:
            copy(pair_up, ups.at[slot], up_send, up_recv, where)

    @pl.when(first)
    def _():
        pl.semaphore_wait(barrier, CUBE - 1 + len(PLANE) + 1)
        others = [column((z + k) % CUBE) for k in range(1, CUBE)]
        for where in others:
            copy(down_ref, tiles.at[mine, slot], z_send, z_recv.at[0], where)
        exchange_ups(others)
        ups[slot] = pair_up[...]
        own_tile.wait()
        wait(slots(mine, 0, CUBE - 1), z_recv.at[0])
        over_plane(0, 0, CUBE)
        wait(slots(mine, CUBE, 2 * CUBE), z_recv.at[1])
        over_plane(1, CUBE, 2 * CUBE)
        for k in (CUBE, 3 * CUBE):
            send(slots(mine, 0, HALF), forward_send, z_recv.at[2], column(z + k))
        wait(slots(mine, 3 * CUBE, CUBE), z_recv.at[2])
        over_plane(2, 3 * CUBE, CUBE)
        send(slots(mine, HALF, HALF), forward_send, z_recv.at[1], column(z + 3 * CUBE))

    @pl.when(second)
    def _():
        pl.semaphore_wait(barrier, CUBE + len(PLANE) + 1)
        others = [column(k) for k in range(CUBE)]
        for where in others:
            copy(down_ref, tiles.at[mine, slot], z_send, z_recv.at[1], where)
        exchange_ups(others)

    @pl.when(last)
    def _():
        pl.semaphore_wait(barrier, HALF + len(PLANE) + 1)
        for k in range(CUBE):
            copy(down_ref, tiles.at[mine, slot], z_send, z_recv.at[1 + slot // (3 * CUBE)], column(k))
        for k in range(CUBE, HALF):
            copy(down_ref, tiles.at[mine, slot], z_send, z_recv.at[1], column(k))
        exchange_ups([column(k) for k in range(HALF)])

    @pl.when(not_first)
    def _():
        for g, start in ((1, HALF), (2, 0)):
            wait(slots(mine, start, HALF), z_recv.at[g])
            over_plane(g, start, HALF)

            @pl.when(second)
            def _():
                send(slots(mine, start, HALF), forward_send, z_recv.at[g], column(z + CUBE))

    def cut(a, count, start, size, which):
        return tiles.at[pl.ds(block_of(a, 0, which), count), pl.ds(start, size)]

    def arrived(a, own, g, start, size):
        wait(cut(a, NY - 1 if own else NY, start, size, core), xy_recv.at[a, g])

    columns = [((x + dx) % NX, dx == 0) for dx in (0, 1, 3, 2)]

    @pl.when(first)
    def _():
        for g, start, size in ((0, 0, CUBE), (1, CUBE, 2 * CUBE)):
            for a, own in columns:
                arrived(a, own, g, start, size)

    @pl.when(not_first)
    def _():
        for a, own in columns:
            arrived(a, own, 1, HALF, HALF)

    leading = jnp.where(first, 0, HALF)
    send(cut(0, NX * NY, leading, HALF, core), core_send.at[0], core_recv.at[NX], partner)

    @pl.when(first)
    def _():
        wait(ups.at[pl.ds(0, NZ - 1)], up_recv)
        send(ups.at[pl.ds(0, HALF)], up_forward_send, up_recv, column(z + CUBE))
        send(ups, up_forward_send, up_recv, column(z + 3 * CUBE))

    @pl.when(not_first)
    def _():
        wait(ups, up_recv)

    @pl.when(second)
    def _():
        send(ups, up_forward_send, up_recv, column(z + CUBE))

    get_index.wait()

    iota = lambda shape, dim: lax.broadcasted_iota(jnp.int32, shape, dim)
    k32 = iota((192, 32), 0) % 64
    owner = exchanged(k32 % 16) * 2 + k32 // 32
    holds = (index[...] == owner).astype(jnp.bfloat16)
    q = iota((32, 64), 1)
    spread = (iota((32, 64), 0) == exchanged(q // 4) * 2 + (q // 2) % 2).astype(jnp.bfloat16)
    k64, q64 = iota((192, 64), 0), iota((192, 64), 1)
    pick = jnp.dot(holds, spread, preferred_element_type=jnp.float32)
    pick = jnp.where(q64 % 2 == (k64 // 16) % 2, pick, 0.0)
    pick_high = jnp.where(k64 < 128, pick, 0.0).astype(jnp.bfloat16)
    pick_low = jnp.where(k64 < 128, 0.0, pick).astype(jnp.bfloat16)
    turned = (MERGE_SCALE * ups[...].reshape(64, LANES)).T
    high = turned.astype(jnp.bfloat16)
    low = (turned - high.astype(jnp.float32)).astype(jnp.bfloat16)
    nt = (((1,), (1,)), ((), ()))
    left[...] = (lax.dot_general(high, pick_high, nt, preferred_element_type=jnp.float32)
                 + lax.dot_general(low, pick_low, nt, preferred_element_type=jnp.float32)).astype(jnp.bfloat16)
    get_weight.wait()

    def merge(a, b_low, which):
        parts = []
        for c in range(4):
            parts.append(jnp.concatenate(
                [tiles[w, :, c * 2 + i, :]
                 for w in (block_of(a, b_low, which), block_of(a, b_low + 2, which)) for i in range(2)], axis=0))
        right = jnp.concatenate(parts, axis=1)
        right_high = right.astype(jnp.bfloat16)
        right_low = (right - right_high.astype(jnp.float32)).astype(jnp.bfloat16)
        right = jnp.concatenate([right_high, right_low, right_high], axis=0)
        update = jnp.dot(left[...], right, preferred_element_type=jnp.float32)
        at = pl.ds(pl.multiple_of(((b_low * NX + a) * 2 + which) * COLUMNS, COLUMNS), COLUMNS)
        out_ref[:, at] = (weight[:, at].astype(jnp.float32) + update).astype(jnp.bfloat16)

    def from_sibling(a):
        wait(cut(a, NY, 0, HALF, 1 - core), core_recv.at[a])
        for b in range(2):
            merge(a, b, 1 - core)

    for n, (a, own) in enumerate(columns):
        @pl.when(first)
        def _():
            arrived(a, own, 2, 3 * CUBE, CUBE)

        @pl.when(not_first)
        def _():
            arrived(a, own, 2, 0, HALF)

        send(cut(a, NY, HALF - leading, HALF, core), core_send.at[1], core_recv.at[a], partner)
        for b in range(2):
            merge(a, b, core)
        if n == 0:
            wait(cut(0, NX * NY, 0, HALF, 1 - core), core_recv.at[NX])
        else:
            from_sibling(columns[n - 1][0])
    from_sibling(columns[-1][0])

    wait(pair_up.at[0], pair_send)

    @pl.when(first)
    def _():
        wait(slots(mine, 0, CUBE - 1), z_send)
        wait(ups.at[pl.ds(0, CUBE - 1)], up_send)
        wait(tiles.at[pl.ds(0, 3), pl.ds(0, HALF)], forward_send)
        wait(slots(mine, 0, 12), up_forward_send)

    @pl.when(second)
    def _():
        wait(slots(mine, 0, CUBE), z_send)
        wait(ups.at[pl.ds(0, CUBE)], up_send)
        wait(tiles.at[mine], forward_send)
        wait(ups, up_forward_send)

    @pl.when(last)
    def _():
        wait(slots(mine, 0, HALF), z_send)
        wait(ups.at[pl.ds(0, HALF)], up_send)

    wait(tiles.at[pl.ds(0, 15)], xy_send)
    for k in range(2):
        wait(cut(0, NX * NY, 0, HALF, core), core_send.at[k])


def local(key_head_weight, down_factor_slots, adapter_up_factor, piece_slot_index):
    units, width = key_head_weight.shape[1:]
    tile = down_factor_slots.reshape(2, 4, LANES).transpose(1, 0, 2).reshape(8, LANES)
    dma = pltpu.SemaphoreType.DMA
    operands = (piece_slot_index.reshape(1, 32), tile, adapter_up_factor, key_head_weight.reshape(units, width))
    merged = pl.pallas_call(
        kernel,
        out_shape=jax.ShapeDtypeStruct((units, width), jnp.bfloat16),
        in_specs=[pl.BlockSpec(memory_space=pltpu.HBM)] * 4,
        out_specs=pl.BlockSpec(memory_space=pltpu.VMEM),
        scratch_shapes=[
            pltpu.VMEM((1, 32), jnp.int32),
            pltpu.VMEM((32, NZ, 8, LANES), jnp.float32),
            pltpu.VMEM((NZ, 2, 2, LANES), jnp.float32),
            pltpu.VMEM((2, 2, LANES), jnp.float32),
            pltpu.VMEM((units, width), jnp.bfloat16),
            pltpu.VMEM((units, 192), jnp.bfloat16),
            dma, dma((3,)), dma, dma((3,)), dma, dma, dma, dma, dma, dma,
            dma, dma((NX, 3)), dma((2,)), dma((NX + 1,)),
        ],
        compiler_params=pltpu.CompilerParams(
            collective_id=0, has_side_effects=True, vmem_limit_bytes=32 << 20),
        name="gather_and_merge",
    )(*[pltpu.with_memory_space_constraint(a, pltpu.HBM) for a in operands])
    return merged.reshape(1, units, width)


def solution(mesh):
    in_specs = (P("tensor", None, None), P("replica", None, "tensor"), P("replica", None), P())
    out_specs = P("tensor", None, None)
    return jax.shard_map(local, mesh=mesh, in_specs=in_specs, out_specs=out_specs, check_vma=False)
```

```python
import jax
import jax.numpy as jnp
from jax import lax
from jax.experimental import pallas as pl
from jax.experimental.pallas import tpu as pltpu
from jax.sharding import PartitionSpec as P

MESH = pl.DeviceIdType.MESH
MERGE_SCALE = 2.0
NX, NY, NZ = 4, 4, 16
CUBE = 4
HALF = 8
LANES = 128
COLUMNS = 512
PLANE = [(2, 2), (2, 1), (2, 3), (1, 2), (3, 2), (1, 1), (1, 3), (3, 1), (3, 3),
         (2, 0), (0, 2), (1, 0), (3, 0), (0, 1), (0, 3)]


def place(x, y, z, core):
    return (z * 2 + y // 2, ((y % 2) * NX + x) * 2 + core)


def block_of(x, y, core):
    return (core * NX + x) * NY + y


def exchanged(z):
    return z + CUBE * (z // HALF) * (1 - 2 * ((z // CUBE) % 2))


def kernel(index_ref, down_ref, up_ref, weight_ref, out_ref, index, tiles, ups, pair_up, weight, left,
           weight_sem, small_sem, z_send, z_recv, pair_send, pair_recv, up_send, up_recv,
           up_late_recv, here, forward_send, up_forward_send, xy_send, xy_recv, core_send, core_recv):
    replica, tensor = lax.axis_index("replica"), lax.axis_index("tensor")
    z, y_hi = replica // 2, replica % 2
    y, x, core = y_hi * 2 + tensor // 8, (tensor // 2) % NX, tensor % 2
    mine, slot = block_of(x, y, core), exchanged(z)
    first, second = z < CUBE, z // CUBE == 1
    last, not_first = z >= HALF, z >= CUBE

    def column(k):
        return place(x, y, k, core)

    plane = [place((x + dx) % NX, (y + dy) % NY, z, core) for dx, dy in PLANE]
    partner = place(x, y, z, 1 - core)

    barrier = pltpu.get_barrier_semaphore()

    def signal(where):
        pl.semaphore_signal(barrier, inc=1, device_id=where, device_id_type=MESH)

    @pl.when(z < HALF)
    def _():
        for k in range(HALF, NZ):
            signal(column(k))

    @pl.when(first)
    def _():
        for k in range(CUBE, HALF):
            signal(column(k))
        for k in range(1, CUBE):
            signal(column((z + k) % CUBE))

    @pl.when(second)
    def _():
        for k in range(1, CUBE):
            signal(column(CUBE + (z + k) % CUBE))

    late_others = [column(HALF + (z + k) % HALF) for k in range(1, HALF)]

    @pl.when(last)
    def _():
        for where in late_others:
            signal(where)

    for where in plane:
        signal(where)
    signal(partner)

    my_up = up_ref.at[:, pl.ds(pl.multiple_of(tensor // 2 * LANES, LANES), LANES)]
    own_tile = pltpu.make_async_copy(down_ref, tiles.at[mine, slot], small_sem.at[0])
    own_up = pltpu.make_async_copy(my_up, pair_up.at[y_hi], small_sem.at[1])
    get_index = pltpu.make_async_copy(index_ref, index, small_sem.at[2])
    get_weight = pltpu.make_async_copy(weight_ref, weight, weight_sem)

    own_tile.start()
    own_up.start()
    get_index.start()
    get_weight.start()

    def copy(source, target, send_sem, recv_sem, where):
        pltpu.make_async_remote_copy(src_ref=source, dst_ref=target, send_sem=send_sem, recv_sem=recv_sem,
                                     device_id=where, device_id_type=MESH).start()

    def send(ref, send_sem, recv_sem, where):
        copy(ref, ref, send_sem, recv_sem, where)

    def wait(ref, sem):
        pltpu.make_async_copy(ref, ref, sem).wait()

    def slots(w, start, size):
        return tiles.at[w, pl.ds(start, size)]

    def over_plane(g, start, size):
        for where in plane:
            send(slots(mine, start, size), xy_send, xy_recv.at[x, g], where)

    def swap_ups():
        copy(my_up, pair_up.at[y_hi], pair_send, pair_recv, place(x, (y + 2) % NY, z, core))

    def send_ups(others, recv_sem):
        own_up.wait()
        wait(pair_up.at[1 - y_hi], pair_recv)
        for where in others:
            copy(pair_up, ups.at[slot], up_send, recv_sem, where)

    early_ups, late_ups = ups.at[pl.ds(0, HALF)], ups.at[pl.ds(HALF, HALF)]

    @pl.when(first)
    def _():
        pl.semaphore_wait(barrier, CUBE - 1 + len(PLANE) + 1)
        others = [column((z + k) % CUBE) for k in range(1, CUBE)]
        for where in others:
            copy(down_ref, tiles.at[mine, slot], z_send, z_recv.at[0], where)
        swap_ups()
        send_ups(others, up_recv)
        ups[slot] = pair_up[...]
        own_tile.wait()
        wait(slots(mine, 0, CUBE - 1), z_recv.at[0])
        over_plane(0, 0, CUBE)
        pl.semaphore_wait(here, 1)
        send(slots(mine, 0, CUBE), forward_send, z_recv.at[0], column(z + CUBE))
        wait(slots(mine, CUBE, CUBE), z_recv.at[1])
        over_plane(1, CUBE, CUBE)
        wait(slots(mine, HALF, CUBE), z_recv.at[2])
        send(slots(mine, 0, HALF), forward_send, z_recv.at[0], column(z + 3 * CUBE))
        over_plane(2, HALF, CUBE)
        wait(slots(mine, 3 * CUBE, CUBE), z_recv.at[3])
        over_plane(3, 3 * CUBE, CUBE)
        wait(ups.at[pl.ds(0, HALF - 1)], up_recv)
        for k in (CUBE, 3 * CUBE):
            send(early_ups, up_forward_send, up_recv, column(z + k))

    @pl.when(second)
    def _():
        pl.semaphore_wait(barrier, HALF - 1 + len(PLANE) + 1)
        pl.semaphore_signal(here, inc=1, device_id=column(z - CUBE), device_id_type=MESH)
        for k in range(CUBE):
            copy(down_ref, tiles.at[mine, slot], z_send, z_recv.at[1], column(k))
        for k in range(1, CUBE):
            copy(down_ref, tiles.at[mine, slot], z_send, z_recv.at[1], column(CUBE + (z + k) % CUBE))
        swap_ups()
        send_ups([column(k) for k in range(CUBE)], up_recv)
        own_tile.wait()
        wait(slots(mine, CUBE, CUBE - 1), z_recv.at[1])
        over_plane(1, CUBE, CUBE)
        wait(slots(mine, HALF, HALF), z_recv.at[2])
        wait(slots(mine, 0, CUBE), z_recv.at[0])
        send(slots(mine, 0, HALF), forward_send, z_recv.at[0], column(z + CUBE))
        over_plane(2, HALF, HALF)
        over_plane(0, 0, CUBE)
        wait(early_ups, up_recv)
        send(early_ups, up_forward_send, up_recv, column(z + CUBE))

    @pl.when(last)
    def _():
        pl.semaphore_wait(barrier, NZ - 1 + len(PLANE) + 1)
        for k in range(CUBE):
            copy(down_ref, tiles.at[mine, slot], z_send, z_recv.at[2 + slot // (3 * CUBE)], column(k))
        for k in range(CUBE, HALF):
            copy(down_ref, tiles.at[mine, slot], z_send, z_recv.at[2], column(k))
        swap_ups()
        for where in late_others:
            copy(down_ref, tiles.at[mine, slot], z_send, z_recv.at[2], where)
        send_ups([column(k) for k in range(HALF)] + late_others, up_late_recv)
        ups[slot] = pair_up[...]
        own_tile.wait()
        wait(slots(mine, HALF, HALF - 1), z_recv.at[2])
        over_plane(2, HALF, HALF)
        wait(slots(mine, 0, HALF), z_recv.at[0])
        over_plane(0, 0, HALF)

    def cut(a, count, start, size, which):
        return tiles.at[pl.ds(block_of(a, 0, which), count), pl.ds(start, size)]

    def arrived(a, own, g, start, size):
        wait(cut(a, NY - 1 if own else NY, start, size, core), xy_recv.at[a, g])

    columns = [((x + dx) % NX, dx == 0) for dx in (0, 1, 3, 2)]

    def arrive(a, own, lead):
        @pl.when(first)
        def _():
            for g in (0, 1) if lead else (2, 3):
                arrived(a, own, g, 0, CUBE)

        @pl.when(not_first)
        def _():
            if lead:
                arrived(a, own, 2, 0, HALF)

        if not lead:
            @pl.when(second)
            def _():
                for g in (1, 0):
                    arrived(a, own, g, 0, CUBE)

            @pl.when(last)
            def _():
                arrived(a, own, 0, 0, HALF)

    for a, own in columns:
        arrive(a, own, True)

    leading = jnp.where(first, 0, HALF)
    send(cut(0, NX * NY, leading, HALF, core), core_send.at[0], core_recv.at[NX], partner)

    @pl.when(z < HALF)
    def _():
        wait(late_ups, up_late_recv)

    @pl.when(last)
    def _():
        wait(early_ups, up_recv)
        wait(ups.at[pl.ds(HALF, HALF - 1)], up_late_recv)

    get_index.wait()

    iota = lambda shape, dim: lax.broadcasted_iota(jnp.int32, shape, dim)
    k32 = iota((192, 32), 0) % 64
    owner = exchanged(k32 % 16) * 2 + k32 // 32
    holds = (index[...] == owner).astype(jnp.bfloat16)
    q = iota((32, 64), 1)
    spread = (iota((32, 64), 0) == exchanged(q // 4) * 2 + (q // 2) % 2).astype(jnp.bfloat16)
    k64, q64 = iota((192, 64), 0), iota((192, 64), 1)
    pick = jnp.dot(holds, spread, preferred_element_type=jnp.float32)
    pick = jnp.where(q64 % 2 == (k64 // 16) % 2, pick, 0.0)
    pick_high = jnp.where(k64 < 128, pick, 0.0).astype(jnp.bfloat16)
    pick_low = jnp.where(k64 < 128, 0.0, pick).astype(jnp.bfloat16)
    turned = (MERGE_SCALE * ups[...].reshape(64, LANES)).T
    high = turned.astype(jnp.bfloat16)
    low = (turned - high.astype(jnp.float32)).astype(jnp.bfloat16)
    nt = (((1,), (1,)), ((), ()))
    left[...] = (lax.dot_general(high, pick_high, nt, preferred_element_type=jnp.float32)
                 + lax.dot_general(low, pick_low, nt, preferred_element_type=jnp.float32)).astype(jnp.bfloat16)
    get_weight.wait()

    def merge(a, b_low, which):
        parts = []
        for c in range(4):
            parts.append(jnp.concatenate(
                [tiles[w, :, c * 2 + i, :]
                 for w in (block_of(a, b_low, which), block_of(a, b_low + 2, which)) for i in range(2)], axis=0))
        right = jnp.concatenate(parts, axis=1)
        right_high = right.astype(jnp.bfloat16)
        right_low = (right - right_high.astype(jnp.float32)).astype(jnp.bfloat16)
        right = jnp.concatenate([right_high, right_low, right_high], axis=0)
        update = jnp.dot(left[...], right, preferred_element_type=jnp.float32)
        at = pl.ds(pl.multiple_of(((b_low * NX + a) * 2 + which) * COLUMNS, COLUMNS), COLUMNS)
        out_ref[:, at] = (weight[:, at].astype(jnp.float32) + update).astype(jnp.bfloat16)

    def from_sibling(a):
        wait(cut(a, NY, 0, HALF, 1 - core), core_recv.at[a])
        for b in range(2):
            merge(a, b, 1 - core)

    for n, (a, own) in enumerate(columns):
        arrive(a, own, False)
        send(cut(a, NY, HALF - leading, HALF, core), core_send.at[1], core_recv.at[a], partner)
        for b in range(2):
            merge(a, b, core)
        if n == 0:
            wait(cut(0, NX * NY, 0, HALF, 1 - core), core_recv.at[NX])
        else:
            from_sibling(columns[n - 1][0])
    from_sibling(columns[-1][0])

    wait(pair_up.at[0], pair_send)

    @pl.when(first)
    def _():
        wait(slots(mine, 0, CUBE - 1), z_send)
        wait(ups.at[pl.ds(0, CUBE - 1)], up_send)
        wait(slots(mine, 0, 3 * CUBE), forward_send)
        wait(ups, up_forward_send)

    @pl.when(second)
    def _():
        wait(slots(mine, 0, HALF - 1), z_send)
        wait(ups.at[pl.ds(0, CUBE)], up_send)
        wait(slots(mine, 0, HALF), forward_send)
        wait(early_ups, up_forward_send)

    @pl.when(last)
    def _():
        wait(slots(mine, 0, NZ - 1), z_send)
        wait(ups.at[pl.ds(0, NZ - 1)], up_send)

    wait(tiles.at[pl.ds(0, 15)], xy_send)
    for k in range(2):
        wait(cut(0, NX * NY, 0, HALF, core), core_send.at[k])


def local(key_head_weight, down_factor_slots, adapter_up_factor, piece_slot_index):
    units, width = key_head_weight.shape[1:]
    tile = down_factor_slots.reshape(2, 4, LANES).transpose(1, 0, 2).reshape(8, LANES)
    dma = pltpu.SemaphoreType.DMA
    operands = (piece_slot_index.reshape(1, 32), tile, adapter_up_factor, key_head_weight.reshape(units, width))
    merged = pl.pallas_call(
        kernel,
        out_shape=jax.ShapeDtypeStruct((units, width), jnp.bfloat16),
        in_specs=[pl.BlockSpec(memory_space=pltpu.HBM)] * 4,
        out_specs=pl.BlockSpec(memory_space=pltpu.VMEM),
        scratch_shapes=[
            pltpu.VMEM((1, 32), jnp.int32),
            pltpu.VMEM((32, NZ, 8, LANES), jnp.float32),
            pltpu.VMEM((NZ, 2, 2, LANES), jnp.float32),
            pltpu.VMEM((2, 2, LANES), jnp.float32),
            pltpu.VMEM((units, width), jnp.bfloat16),
            pltpu.VMEM((units, 192), jnp.bfloat16),
            dma, dma((3,)), dma, dma((4,)), dma, dma, dma, dma,
            dma, pltpu.SemaphoreType.REGULAR, dma, dma, dma, dma((NX, 4)), dma((2,)), dma((NX + 1,)),
        ],
        compiler_params=pltpu.CompilerParams(
            collective_id=0, has_side_effects=True, vmem_limit_bytes=32 << 20),
        name="gather_and_merge",
    )(*[pltpu.with_memory_space_constraint(a, pltpu.HBM) for a in operands])
    return merged.reshape(1, units, width)


def solution(mesh):
    in_specs = (P("tensor", None, None), P("replica", None, "tensor"), P("replica", None), P())
    out_specs = P("tensor", None, None)
    return jax.shard_map(local, mesh=mesh, in_specs=in_specs, out_specs=out_specs, check_vma=False)
```

```python
import jax
import jax.numpy as jnp
from jax import lax
from jax.experimental import pallas as pl
from jax.experimental.pallas import tpu as pltpu
from jax.sharding import PartitionSpec as P

MESH = pl.DeviceIdType.MESH
MERGE_SCALE = 2.0
NX, NY, NZ = 4, 4, 16
CUBE = 4
HALF = 8
LANES = 128
COLUMNS = 512
PLANE = [(2, 2), (2, 1), (2, 3), (1, 2), (3, 2), (1, 1), (1, 3), (3, 1), (3, 3),
         (2, 0), (0, 2), (1, 0), (3, 0), (0, 1), (0, 3)]


def place(x, y, z, core):
    return (z * 2 + y // 2, ((y % 2) * NX + x) * 2 + core)


def block_of(x, y, core):
    return (core * NX + x) * NY + y


def exchanged(z):
    return z + CUBE * (z // HALF) * (1 - 2 * ((z // CUBE) % 2))


def kernel(index_ref, down_ref, up_ref, weight_ref, out_ref, index, tiles, ups, pair_up, weight, left,
           weight_sem, small_sem, z_send, z_recv, pair_send, pair_recv, up_send, up_recv,
           up_late_recv, here, forward_send, up_forward_send, xy_send, xy_recv, core_send, core_recv):
    replica, tensor = lax.axis_index("replica"), lax.axis_index("tensor")
    z, y_hi = replica // 2, replica % 2
    y, x, core = y_hi * 2 + tensor // 8, (tensor // 2) % NX, tensor % 2
    mine, slot = block_of(x, y, core), exchanged(z)
    first, second = z < CUBE, z // CUBE == 1
    last = z >= HALF

    def column(k):
        return place(x, y, k, core)

    plane = [place((x + dx) % NX, (y + dy) % NY, z, core) for dx, dy in PLANE]
    partner = place(x, y, z, 1 - core)

    barrier = pltpu.get_barrier_semaphore()

    def signal(where):
        pl.semaphore_signal(barrier, inc=1, device_id=where, device_id_type=MESH)

    late_others = [column(HALF + (z + k) % HALF) for k in (4, 5, 3, 6, 2, 7, 1)]

    @pl.when(last)
    def _():
        for where in late_others:
            signal(where)

    @pl.when(z < HALF)
    def _():
        for k in range(1, CUBE):
            signal(column(z // CUBE * CUBE + (z + k) % CUBE))

    for where in plane:
        signal(where)
    signal(partner)

    @pl.when(first)
    def _():
        for k in range(CUBE, HALF):
            signal(column(k))

    @pl.when(z < HALF)
    def _():
        for k in range(HALF, NZ):
            signal(column(k))

    my_up = up_ref.at[:, pl.ds(pl.multiple_of(tensor // 2 * LANES, LANES), LANES)]
    own_tile = pltpu.make_async_copy(down_ref, tiles.at[mine, slot], small_sem.at[0])
    own_up = pltpu.make_async_copy(my_up, pair_up.at[y_hi], small_sem.at[1])
    get_index = pltpu.make_async_copy(index_ref, index, small_sem.at[2])
    get_weight = pltpu.make_async_copy(weight_ref, weight, weight_sem)

    own_tile.start()
    own_up.start()
    get_index.start()
    get_weight.start()

    def copy(source, target, send_sem, recv_sem, where):
        pltpu.make_async_remote_copy(src_ref=source, dst_ref=target, send_sem=send_sem, recv_sem=recv_sem,
                                     device_id=where, device_id_type=MESH).start()

    def send(ref, send_sem, recv_sem, where):
        copy(ref, ref, send_sem, recv_sem, where)

    def wait(ref, sem):
        pltpu.make_async_copy(ref, ref, sem).wait()

    def slots(w, start, size):
        return tiles.at[w, pl.ds(start, size)]

    def over_plane(g, start, size):
        for where in plane:
            send(slots(mine, start, size), xy_send, xy_recv.at[x, g], where)

    own_tile.wait()

    def swap_ups():
        copy(my_up, pair_up.at[y_hi], pair_send, pair_recv, place(x, (y + 2) % NY, z, core))

    def send_ups(others, recv_sem):
        own_up.wait()
        wait(pair_up.at[1 - y_hi], pair_recv)
        for where in others:
            copy(pair_up, ups.at[slot], up_send, recv_sem, where)

    early_ups, late_ups = ups.at[pl.ds(0, HALF)], ups.at[pl.ds(HALF, HALF)]

    @pl.when(first)
    def _():
        pl.semaphore_wait(barrier, CUBE - 1 + len(PLANE) + 1)
        others = [column((z + k) % CUBE) for k in range(1, CUBE)]
        for where in others:
            send(tiles.at[mine, slot], z_send, z_recv.at[0], where)
        swap_ups()
        send_ups(others, up_recv)
        ups[slot] = pair_up[...]
        wait(slots(mine, 0, CUBE - 1), z_recv.at[0])
        over_plane(0, 0, CUBE)
        pl.semaphore_wait(here, 1)
        send(slots(mine, 0, CUBE), forward_send, z_recv.at[0], column(z + CUBE))
        wait(slots(mine, CUBE, CUBE), z_recv.at[1])
        over_plane(1, CUBE, CUBE)
        wait(slots(mine, HALF, CUBE), z_recv.at[2])
        send(slots(mine, 0, HALF), forward_send, z_recv.at[0], column(z + 3 * CUBE))
        over_plane(2, HALF, CUBE)
        wait(slots(mine, 3 * CUBE, CUBE), z_recv.at[3])
        over_plane(3, 3 * CUBE, CUBE)
        wait(ups.at[pl.ds(0, HALF - 1)], up_recv)
        for k in (CUBE, 3 * CUBE):
            send(early_ups, up_forward_send, up_recv, column(z + k))

    @pl.when(second)
    def _():
        pl.semaphore_wait(barrier, HALF - 1 + len(PLANE) + 1)
        pl.semaphore_signal(here, inc=1, device_id=column(z - CUBE), device_id_type=MESH)
        for k in range(CUBE):
            send(tiles.at[mine, slot], z_send, z_recv.at[1], column(k))
        for k in range(1, CUBE):
            send(tiles.at[mine, slot], z_send, z_recv.at[1], column(CUBE + (z + k) % CUBE))
        swap_ups()
        send_ups([column(k) for k in range(CUBE)], up_recv)
        wait(slots(mine, CUBE, CUBE - 1), z_recv.at[1])
        over_plane(1, CUBE, CUBE)
        wait(slots(mine, 3 * CUBE, CUBE), z_recv.at[3])
        wait(slots(mine, 0, CUBE), z_recv.at[0])
        send(slots(mine, 0, HALF), forward_send, z_recv.at[0], column(z + CUBE))
        over_plane(0, 0, CUBE)
        over_plane(3, 3 * CUBE, CUBE)
        wait(slots(mine, HALF, CUBE), z_recv.at[2])
        over_plane(2, HALF, CUBE)
        wait(early_ups, up_recv)
        send(early_ups, up_forward_send, up_recv, column(z + CUBE))

    @pl.when(last)
    def _():
        pl.semaphore_wait(barrier, NZ - 1 + len(PLANE) + 1)
        swap_ups()
        for k in range(HALF):
            send(tiles.at[mine, slot], z_send, z_recv.at[2 + slot // (3 * CUBE)], column(k))
        for where in late_others:
            send(tiles.at[mine, slot], z_send, z_recv.at[2], where)
        send_ups([column(k) for k in range(HALF)] + late_others, up_late_recv)
        ups[slot] = pair_up[...]
        wait(slots(mine, HALF, HALF - 1), z_recv.at[2])
        over_plane(2, HALF, HALF)
        wait(slots(mine, 0, HALF), z_recv.at[0])
        over_plane(0, 0, HALF)

    def cut(a, count, start, size, which):
        return tiles.at[pl.ds(block_of(a, 0, which), count), pl.ds(start, size)]

    def arrived(a, own, g, start, size):
        wait(cut(a, NY - 1 if own else NY, start, size, core), xy_recv.at[a, g])

    columns = [((x + dx) % NX, dx == 0) for dx in (0, 1, 3, 2)]

    def arrive(a, own, lead):
        @pl.when(z < HALF)
        def _():
            for g in (0, 1) if lead else (2, 3):
                arrived(a, own, g, 0, CUBE)

        @pl.when(last)
        def _():
            arrived(a, own, 2 if lead else 0, 0, HALF)

    for a, own in columns:
        arrive(a, own, True)

    leading = jnp.where(last, HALF, 0)
    send(cut(0, NX * NY, leading, HALF, core), core_send.at[0], core_recv.at[NX], partner)

    @pl.when(z < HALF)
    def _():
        wait(late_ups, up_late_recv)

    @pl.when(last)
    def _():
        wait(early_ups, up_recv)
        wait(ups.at[pl.ds(HALF, HALF - 1)], up_late_recv)

    get_index.wait()

    iota = lambda shape, dim: lax.broadcasted_iota(jnp.int32, shape, dim)
    k32 = iota((192, 32), 0) % 64
    owner = exchanged(k32 % 16) * 2 + k32 // 32
    holds = (index[...] == owner).astype(jnp.bfloat16)
    q = iota((32, 64), 1)
    spread = (iota((32, 64), 0) == exchanged(q // 4) * 2 + (q // 2) % 2).astype(jnp.bfloat16)
    k64, q64 = iota((192, 64), 0), iota((192, 64), 1)
    pick = jnp.dot(holds, spread, preferred_element_type=jnp.float32)
    pick = jnp.where(q64 % 2 == (k64 // 16) % 2, pick, 0.0)
    pick_high = jnp.where(k64 < 128, pick, 0.0).astype(jnp.bfloat16)
    pick_low = jnp.where(k64 < 128, 0.0, pick).astype(jnp.bfloat16)
    turned = (MERGE_SCALE * ups[...].reshape(64, LANES)).T
    high = turned.astype(jnp.bfloat16)
    low = (turned - high.astype(jnp.float32)).astype(jnp.bfloat16)
    nt = (((1,), (1,)), ((), ()))
    left[...] = (lax.dot_general(high, pick_high, nt, preferred_element_type=jnp.float32)
                 + lax.dot_general(low, pick_low, nt, preferred_element_type=jnp.float32)).astype(jnp.bfloat16)
    get_weight.wait()

    def merge(a, b_low, which):
        parts = []
        for c in range(4):
            parts.append(jnp.concatenate(
                [tiles[w, :, c * 2 + i, :]
                 for w in (block_of(a, b_low, which), block_of(a, b_low + 2, which)) for i in range(2)], axis=0))
        right = jnp.concatenate(parts, axis=1)
        right_high = right.astype(jnp.bfloat16)
        right_low = (right - right_high.astype(jnp.float32)).astype(jnp.bfloat16)
        right = jnp.concatenate([right_high, right_low, right_high], axis=0)
        update = jnp.dot(left[...], right, preferred_element_type=jnp.float32)
        at = pl.ds(pl.multiple_of(((b_low * NX + a) * 2 + which) * COLUMNS, COLUMNS), COLUMNS)
        out_ref[:, at] = (weight[:, at].astype(jnp.float32) + update).astype(jnp.bfloat16)

    def from_sibling(a):
        wait(cut(a, NY, 0, HALF, 1 - core), core_recv.at[a])
        for b in range(2):
            merge(a, b, 1 - core)

    def hand_over(n):
        a, own = columns[n]
        arrive(a, own, False)
        send(cut(a, NY, HALF - leading, HALF, core), core_send.at[1], core_recv.at[a], partner)

    def merge_own(n):
        for b in range(2):
            merge(columns[n][0], b, core)

    def merge_other(n):
        if n == 0:
            wait(cut(0, NX * NY, 0, HALF, 1 - core), core_recv.at[NX])
        wait(cut(columns[n][0], NY, 0, HALF, 1 - core), core_recv.at[columns[n][0]])
        for b in range(2):
            merge(columns[n][0], b, 1 - core)

    for n in range(NX):
        hand_over(n)

    merge_own(0)
    merge_own(1)
    merge_own(2)
    merge_own(3)
    merge_other(0)
    merge_other(1)
    merge_other(2)
    merge_other(3)

    wait(pair_up.at[0], pair_send)

    @pl.when(first)
    def _():
        wait(slots(mine, 0, CUBE - 1), z_send)
        wait(ups.at[pl.ds(0, CUBE - 1)], up_send)
        wait(slots(mine, 0, 3 * CUBE), forward_send)
        wait(ups, up_forward_send)

    @pl.when(second)
    def _():
        wait(slots(mine, 0, HALF - 1), z_send)
        wait(ups.at[pl.ds(0, CUBE)], up_send)
        wait(slots(mine, 0, HALF), forward_send)
        wait(early_ups, up_forward_send)

    @pl.when(last)
    def _():
        wait(slots(mine, 0, NZ - 1), z_send)
        wait(ups.at[pl.ds(0, NZ - 1)], up_send)

    wait(tiles.at[pl.ds(0, 15)], xy_send)
    for k in range(2):
        wait(cut(0, NX * NY, 0, HALF, core), core_send.at[k])


def local(key_head_weight, down_factor_slots, adapter_up_factor, piece_slot_index):
    units, width = key_head_weight.shape[1:]
    tile = down_factor_slots.reshape(2, 4, LANES).transpose(1, 0, 2).reshape(8, LANES)
    dma = pltpu.SemaphoreType.DMA
    operands = (piece_slot_index.reshape(1, 32), tile, adapter_up_factor, key_head_weight.reshape(units, width))
    merged = pl.pallas_call(
        kernel,
        out_shape=jax.ShapeDtypeStruct((units, width), jnp.bfloat16),
        in_specs=[pl.BlockSpec(memory_space=pltpu.HBM)] * 4,
        out_specs=pl.BlockSpec(memory_space=pltpu.VMEM),
        scratch_shapes=[
            pltpu.VMEM((1, 32), jnp.int32),
            pltpu.VMEM((32, NZ, 8, LANES), jnp.float32),
            pltpu.VMEM((NZ, 2, 2, LANES), jnp.float32),
            pltpu.VMEM((2, 2, LANES), jnp.float32),
            pltpu.VMEM((units, width), jnp.bfloat16),
            pltpu.VMEM((units, 192), jnp.bfloat16),
            dma, dma((3,)), dma, dma((4,)), dma, dma, dma, dma,
            dma, pltpu.SemaphoreType.REGULAR, dma, dma, dma, dma((NX, 4)), dma((2,)), dma((NX + 1,)),
        ],
        compiler_params=pltpu.CompilerParams(
            collective_id=0, has_side_effects=True, vmem_limit_bytes=32 << 20),
        name="gather_and_merge",
    )(*[pltpu.with_memory_space_constraint(a, pltpu.HBM) for a in operands])
    return merged.reshape(1, units, width)


def solution(mesh):
    in_specs = (P("tensor", None, None), P("replica", None, "tensor"), P("replica", None), P())
    out_specs = P("tensor", None, None)
    return jax.shard_map(local, mesh=mesh, in_specs=in_specs, out_specs=out_specs, check_vma=False)
```

```python
import jax
import jax.numpy as jnp
from jax import lax
from jax.experimental import pallas as pl
from jax.experimental.pallas import tpu as pltpu
from jax.sharding import PartitionSpec as P

MESH = pl.DeviceIdType.MESH
MERGE_SCALE = 2.0
NX, NY, NZ = 4, 4, 16
CUBE = 4
HALF = 8
LANES = 128
COLUMNS = 512
PLANE = [(2, 2), (1, 2), (2, 1), (1, 1), (2, 0), (0, 2), (1, 0), (0, 1),
         (2, 3), (3, 2), (1, 3), (3, 1), (3, 3), (3, 0), (0, 3)]


def place(x, y, z, core):
    return (z * 2 + y // 2, ((y % 2) * NX + x) * 2 + core)


def block_of(x, y, core):
    return (core * NX + x) * NY + y


def exchanged(z):
    return z + CUBE * (z // HALF) * (1 - 2 * ((z // CUBE) % 2))


def kernel(index_ref, down_ref, up_ref, weight_ref, out_ref, index, tiles, ups, pair_up, weight, left,
           weight_sem, small_sem, z_send, z_recv, pair_send, pair_recv, up_send, up_recv,
           up_late_recv, here, forward_send, up_forward_send, xy_send, xy_recv, turn_recv, core_send, core_recv):
    replica, tensor = lax.axis_index("replica"), lax.axis_index("tensor")
    z, y_hi = replica // 2, replica % 2
    y, x, core = y_hi * 2 + tensor // 8, (tensor // 2) % NX, tensor % 2
    mine, slot = block_of(x, y, core), exchanged(z)
    first, second = z < CUBE, z // CUBE == 1
    last = z >= HALF

    def column(k):
        return place(x, y, k, core)

    plane = [place((x + dx) % NX, (y + dy) % NY, z, core) for dx, dy in PLANE]
    partner = place(x, y, z, 1 - core)

    barrier = pltpu.get_barrier_semaphore()

    def signal(where):
        pl.semaphore_signal(barrier, inc=1, device_id=where, device_id_type=MESH)

    late_others = [column(HALF + (z + k) % HALF) for k in (4, 5, 3, 6, 2, 7, 1)]

    @pl.when(last)
    def _():
        for where in late_others:
            signal(where)

    @pl.when(z < HALF)
    def _():
        for k in range(1, CUBE):
            signal(column(z // CUBE * CUBE + (z + k) % CUBE))

    for where in plane:
        signal(where)
    signal(partner)

    @pl.when(first)
    def _():
        for k in range(CUBE, HALF):
            signal(column(k))

    @pl.when(z < HALF)
    def _():
        for k in range(HALF, NZ):
            signal(column(k))

    my_up = up_ref.at[:, pl.ds(pl.multiple_of(tensor // 2 * LANES, LANES), LANES)]
    own_tile = pltpu.make_async_copy(down_ref, tiles.at[mine, slot], small_sem.at[0])
    own_up = pltpu.make_async_copy(my_up, pair_up.at[y_hi], small_sem.at[1])
    get_index = pltpu.make_async_copy(index_ref, index, small_sem.at[2])
    get_weight = pltpu.make_async_copy(weight_ref, weight, weight_sem)

    own_tile.start()
    own_up.start()
    get_index.start()
    get_weight.start()

    def copy(source, target, send_sem, recv_sem, where):
        pltpu.make_async_remote_copy(src_ref=source, dst_ref=target, send_sem=send_sem, recv_sem=recv_sem,
                                     device_id=where, device_id_type=MESH).start()

    def send(ref, send_sem, recv_sem, where):
        copy(ref, ref, send_sem, recv_sem, where)

    def wait(ref, sem):
        pltpu.make_async_copy(ref, ref, sem).wait()

    def slots(w, start, size):
        return tiles.at[w, pl.ds(start, size)]

    def over_plane(g, start, size):
        for where in plane:
            send(slots(mine, start, size), xy_send, xy_recv.at[x, g], where)

    own_tile.wait()

    turns = (1, 2, 3)
    across = [(x + d) % NX for d in turns]
    along = [(y + d) % NY for d in turns]
    x_others = [place(a, y, z, core) for a in across]
    y_others = [place(x, b, z, core) for b in along]

    def spread(g, start):
        for where in x_others:
            send(slots(mine, start, CUBE), xy_send, turn_recv.at[x] if g == 1 else xy_recv.at[x, g], where)
        for where in y_others:
            send(slots(mine, start, CUBE), xy_send, turn_recv.at[NX + y] if g == 2 else xy_recv.at[x, g], where)

    def pass_on(g, start):
        for n in range(3):
            a, b = (across[n], y) if g == 1 else (x, along[n])
            w = block_of(a, b, core)
            wait(slots(w, start, CUBE), turn_recv.at[across[n] if g == 1 else NX + along[n]])
            for where in y_others if g == 1 else x_others:
                send(slots(w, start, CUBE), xy_send, xy_recv.at[a, g], where)

    def swap_ups():
        copy(my_up, pair_up.at[y_hi], pair_send, pair_recv, place(x, (y + 2) % NY, z, core))

    def send_ups(others, recv_sem):
        own_up.wait()
        wait(pair_up.at[1 - y_hi], pair_recv)
        for where in others:
            copy(pair_up, ups.at[slot], up_send, recv_sem, where)

    early_ups, late_ups = ups.at[pl.ds(0, HALF)], ups.at[pl.ds(HALF, HALF)]

    @pl.when(first)
    def _():
        pl.semaphore_wait(barrier, CUBE - 1 + len(PLANE) + 1)
        others = [column((z + k) % CUBE) for k in range(1, CUBE)]
        for where in others:
            send(tiles.at[mine, slot], z_send, z_recv.at[0], where)
        swap_ups()
        send_ups(others, up_recv)
        ups[slot] = pair_up[...]
        wait(slots(mine, 0, CUBE - 1), z_recv.at[0])
        over_plane(0, 0, CUBE)
        pl.semaphore_wait(here, 1)
        send(slots(mine, 0, CUBE), forward_send, z_recv.at[0], column(z + CUBE))
        wait(slots(mine, CUBE, CUBE), z_recv.at[1])
        spread(1, CUBE)
        wait(slots(mine, HALF, CUBE), z_recv.at[2])
        send(slots(mine, 0, HALF), forward_send, z_recv.at[0], column(z + 3 * CUBE))
        spread(2, HALF)
        pass_on(1, CUBE)
        wait(slots(mine, 3 * CUBE, CUBE), z_recv.at[3])
        over_plane(3, 3 * CUBE, CUBE)
        pass_on(2, HALF)
        wait(ups.at[pl.ds(0, HALF - 1)], up_recv)
        for k in (CUBE, 3 * CUBE):
            send(early_ups, up_forward_send, up_recv, column(z + k))

    @pl.when(second)
    def _():
        pl.semaphore_wait(barrier, HALF - 1 + len(PLANE) + 1)
        pl.semaphore_signal(here, inc=1, device_id=column(z - CUBE), device_id_type=MESH)
        for k in range(CUBE):
            send(tiles.at[mine, slot], z_send, z_recv.at[1], column(k))
        for k in range(1, CUBE):
            send(tiles.at[mine, slot], z_send, z_recv.at[1], column(CUBE + (z + k) % CUBE))
        swap_ups()
        send_ups([column(k) for k in range(CUBE)], up_recv)
        wait(slots(mine, CUBE, CUBE - 1), z_recv.at[1])
        over_plane(1, CUBE, CUBE)
        wait(slots(mine, 3 * CUBE, CUBE), z_recv.at[3])
        wait(slots(mine, 0, CUBE), z_recv.at[0])
        send(slots(mine, 0, HALF), forward_send, z_recv.at[0], column(z + CUBE))
        over_plane(0, 0, CUBE)
        over_plane(3, 3 * CUBE, CUBE)
        wait(slots(mine, HALF, CUBE), z_recv.at[2])
        over_plane(2, HALF, CUBE)
        wait(early_ups, up_recv)
        send(early_ups, up_forward_send, up_recv, column(z + CUBE))

    @pl.when(last)
    def _():
        pl.semaphore_wait(barrier, NZ - 1 + len(PLANE) + 1)
        swap_ups()
        for k in range(HALF):
            send(tiles.at[mine, slot], z_send, z_recv.at[2 + slot // (3 * CUBE)], column(k))
        for where in late_others:
            send(tiles.at[mine, slot], z_send, z_recv.at[2], where)
        send_ups([column(k) for k in range(HALF)] + late_others, up_late_recv)
        ups[slot] = pair_up[...]
        wait(slots(mine, HALF, HALF - 1), z_recv.at[2])
        over_plane(2, HALF, HALF)
        wait(slots(mine, 0, HALF), z_recv.at[0])
        over_plane(0, 0, HALF)

    def cut(a, count, start, size, which):
        return tiles.at[pl.ds(block_of(a, 0, which), count), pl.ds(start, size)]

    def arrived(a, own, g, start, size):
        wait(cut(a, NY - 1 if own else NY, start, size, core), xy_recv.at[a, g])

    columns = [((x + dx) % NX, dx == 0) for dx in (0, 1, 3, 2)]

    def arrive(a, own, lead):
        @pl.when(first)
        def _():
            if lead:
                arrived(a, own, 0, 0, CUBE)
                arrived(a, True, 1, 0, CUBE)
            else:
                if not own:
                    arrived(a, False, 2, 0, CUBE)
                arrived(a, own, 3, 0, CUBE)

        @pl.when(second)
        def _():
            for g in (0, 1) if lead else (2, 3):
                arrived(a, own, g, 0, CUBE)

        @pl.when(last)
        def _():
            arrived(a, own, 2 if lead else 0, 0, HALF)

    for a, own in columns:
        arrive(a, own, True)

    leading = jnp.where(last, HALF, 0)
    send(cut(0, NX * NY, leading, HALF, core), core_send.at[0], core_recv.at[NX], partner)

    @pl.when(z < HALF)
    def _():
        wait(late_ups, up_late_recv)

    @pl.when(last)
    def _():
        wait(early_ups, up_recv)
        wait(ups.at[pl.ds(HALF, HALF - 1)], up_late_recv)

    get_index.wait()

    iota = lambda shape, dim: lax.broadcasted_iota(jnp.int32, shape, dim)
    k32 = iota((192, 32), 0) % 64
    owner = exchanged(k32 % 16) * 2 + k32 // 32
    holds = (index[...] == owner).astype(jnp.bfloat16)
    q = iota((32, 64), 1)
    spread = (iota((32, 64), 0) == exchanged(q // 4) * 2 + (q // 2) % 2).astype(jnp.bfloat16)
    k64, q64 = iota((192, 64), 0), iota((192, 64), 1)
    pick = jnp.dot(holds, spread, preferred_element_type=jnp.float32)
    pick = jnp.where(q64 % 2 == (k64 // 16) % 2, pick, 0.0)
    pick_high = jnp.where(k64 < 128, pick, 0.0).astype(jnp.bfloat16)
    pick_low = jnp.where(k64 < 128, 0.0, pick).astype(jnp.bfloat16)
    turned = (MERGE_SCALE * ups[...].reshape(64, LANES)).T
    high = turned.astype(jnp.bfloat16)
    low = (turned - high.astype(jnp.float32)).astype(jnp.bfloat16)
    nt = (((1,), (1,)), ((), ()))
    left[...] = (lax.dot_general(high, pick_high, nt, preferred_element_type=jnp.float32)
                 + lax.dot_general(low, pick_low, nt, preferred_element_type=jnp.float32)).astype(jnp.bfloat16)
    get_weight.wait()

    def merge(a, b_low, which):
        parts = []
        for c in range(4):
            parts.append(jnp.concatenate(
                [tiles[w, :, c * 2 + i, :]
                 for w in (block_of(a, b_low, which), block_of(a, b_low + 2, which)) for i in range(2)], axis=0))
        right = jnp.concatenate(parts, axis=1)
        right_high = right.astype(jnp.bfloat16)
        right_low = (right - right_high.astype(jnp.float32)).astype(jnp.bfloat16)
        right = jnp.concatenate([right_high, right_low, right_high], axis=0)
        update = jnp.dot(left[...], right, preferred_element_type=jnp.float32)
        at = pl.ds(pl.multiple_of(((b_low * NX + a) * 2 + which) * COLUMNS, COLUMNS), COLUMNS)
        out_ref[:, at] = (weight[:, at].astype(jnp.float32) + update).astype(jnp.bfloat16)

    def from_sibling(a):
        wait(cut(a, NY, 0, HALF, 1 - core), core_recv.at[a])
        for b in range(2):
            merge(a, b, 1 - core)

    def hand_over(n):
        a, own = columns[n]
        arrive(a, own, False)
        send(cut(a, NY, HALF - leading, HALF, core), core_send.at[1], core_recv.at[a], partner)

    def merge_own(n):
        for b in range(2):
            merge(columns[n][0], b, core)

    def merge_other(n):
        if n == 0:
            wait(cut(0, NX * NY, 0, HALF, 1 - core), core_recv.at[NX])
        wait(cut(columns[n][0], NY, 0, HALF, 1 - core), core_recv.at[columns[n][0]])
        for b in range(2):
            merge(columns[n][0], b, 1 - core)

    for n in range(NX):
        hand_over(n)

    merge_own(0)
    merge_own(1)
    merge_own(2)
    merge_own(3)
    merge_other(0)
    merge_other(1)
    merge_other(2)
    merge_other(3)

    wait(pair_up.at[0], pair_send)

    @pl.when(first)
    def _():
        wait(slots(mine, 0, CUBE - 1), z_send)
        wait(ups.at[pl.ds(0, CUBE - 1)], up_send)
        wait(slots(mine, 0, 3 * CUBE), forward_send)
        wait(ups, up_forward_send)

    @pl.when(second)
    def _():
        wait(slots(mine, 0, HALF - 1), z_send)
        wait(ups.at[pl.ds(0, CUBE)], up_send)
        wait(slots(mine, 0, HALF), forward_send)
        wait(early_ups, up_forward_send)

    @pl.when(last)
    def _():
        wait(slots(mine, 0, NZ - 1), z_send)
        wait(ups.at[pl.ds(0, NZ - 1)], up_send)

    wait(tiles.at[pl.ds(0, 15)], xy_send)
    for k in range(2):
        wait(cut(0, NX * NY, 0, HALF, core), core_send.at[k])


def local(key_head_weight, down_factor_slots, adapter_up_factor, piece_slot_index):
    units, width = key_head_weight.shape[1:]
    tile = down_factor_slots.reshape(2, 4, LANES).transpose(1, 0, 2).reshape(8, LANES)
    dma = pltpu.SemaphoreType.DMA
    operands = (piece_slot_index.reshape(1, 32), tile, adapter_up_factor, key_head_weight.reshape(units, width))
    merged = pl.pallas_call(
        kernel,
        out_shape=jax.ShapeDtypeStruct((units, width), jnp.bfloat16),
        in_specs=[pl.BlockSpec(memory_space=pltpu.HBM)] * 4,
        out_specs=pl.BlockSpec(memory_space=pltpu.VMEM),
        scratch_shapes=[
            pltpu.VMEM((1, 32), jnp.int32),
            pltpu.VMEM((32, NZ, 8, LANES), jnp.float32),
            pltpu.VMEM((NZ, 2, 2, LANES), jnp.float32),
            pltpu.VMEM((2, 2, LANES), jnp.float32),
            pltpu.VMEM((units, width), jnp.bfloat16),
            pltpu.VMEM((units, 192), jnp.bfloat16),
            dma, dma((3,)), dma, dma((4,)), dma, dma, dma, dma,
            dma, pltpu.SemaphoreType.REGULAR, dma, dma, dma, dma((NX, 4)), dma((NX + NY,)), dma((2,)), dma((NX + 1,)),
        ],
        compiler_params=pltpu.CompilerParams(
            collective_id=0, has_side_effects=True, vmem_limit_bytes=32 << 20),
        name="gather_and_merge",
    )(*[pltpu.with_memory_space_constraint(a, pltpu.HBM) for a in operands])
    return merged.reshape(1, units, width)


def solution(mesh):
    in_specs = (P("tensor", None, None), P("replica", None, "tensor"), P("replica", None), P())
    out_specs = P("tensor", None, None)
    return jax.shard_map(local, mesh=mesh, in_specs=in_specs, out_specs=out_specs, check_vma=False)
```

```python
import jax
import jax.numpy as jnp
from jax import lax
from jax.experimental import pallas as pl
from jax.experimental.pallas import tpu as pltpu
from jax.sharding import PartitionSpec as P

MESH = pl.DeviceIdType.MESH
MERGE_SCALE = 2.0
NX, NY, NZ = 4, 4, 16
CUBE = 4
HALF = 8
LANES = 128
COLUMNS = 512
PLANE = [(2, 2), (2, 1), (2, 3), (1, 2), (3, 2), (1, 1), (1, 3), (3, 1), (3, 3),
         (2, 0), (0, 2), (1, 0), (3, 0), (0, 1), (0, 3)]


def place(x, y, z, core):
    return (z * 2 + y // 2, ((y % 2) * NX + x) * 2 + core)


def block_of(x, y, core):
    return (core * NX + x) * NY + y


def exchanged(z):
    return z + CUBE * (z // HALF) * (1 - 2 * ((z // CUBE) % 2))


def kernel(index_ref, down_ref, up_ref, weight_ref, out_ref, index, tiles, ups, pair_up, weight, left,
           weight_sem, small_sem, z_send, z_recv, pair_send, pair_recv, up_send, up_recv,
           up_late_recv, here, forward_send, up_forward_send, xy_send, xy_recv, core_send, core_recv):
    replica, tensor = lax.axis_index("replica"), lax.axis_index("tensor")
    z, y_hi = replica // 2, replica % 2
    y, x, core = y_hi * 2 + tensor // 8, (tensor // 2) % NX, tensor % 2
    mine, slot = block_of(x, y, core), exchanged(z)
    first, second = z < CUBE, z // CUBE == 1
    last = z >= HALF

    def column(k):
        return place(x, y, k, core)

    plane = [place((x + dx) % NX, (y + dy) % NY, z, core) for dx, dy in PLANE]
    partner = place(x, y, z, 1 - core)

    barrier = pltpu.get_barrier_semaphore()

    def signal(where):
        pl.semaphore_signal(barrier, inc=1, device_id=where, device_id_type=MESH)

    late_others = [column(HALF + (z + k) % HALF) for k in (4, 5, 3, 6, 2, 7, 1)]

    @pl.when(last)
    def _():
        for where in late_others:
            signal(where)

    @pl.when(z < HALF)
    def _():
        for k in range(1, CUBE):
            signal(column(z // CUBE * CUBE + (z + k) % CUBE))

    for where in plane:
        signal(where)
    signal(partner)

    @pl.when(first)
    def _():
        for k in range(CUBE, HALF):
            signal(column(k))

    @pl.when(z < HALF)
    def _():
        for k in range(HALF, NZ):
            signal(column(k))

    my_up = up_ref.at[:, pl.ds(pl.multiple_of(tensor // 2 * LANES, LANES), LANES)]
    own_tile = pltpu.make_async_copy(down_ref, tiles.at[mine, slot], small_sem.at[0])
    own_up = pltpu.make_async_copy(my_up, pair_up.at[y_hi], small_sem.at[1])
    get_index = pltpu.make_async_copy(index_ref, index, small_sem.at[2])
    get_weight = pltpu.make_async_copy(weight_ref, weight, weight_sem)

    own_tile.start()
    own_up.start()
    get_index.start()
    get_weight.start()

    def copy(source, target, send_sem, recv_sem, where):
        pltpu.make_async_remote_copy(src_ref=source, dst_ref=target, send_sem=send_sem, recv_sem=recv_sem,
                                     device_id=where, device_id_type=MESH).start()

    def send(ref, send_sem, recv_sem, where):
        copy(ref, ref, send_sem, recv_sem, where)

    def wait(ref, sem):
        pltpu.make_async_copy(ref, ref, sem).wait()

    def slots(w, start, size):
        return tiles.at[w, pl.ds(start, size)]

    def over_plane(g, start, size):
        for where in plane:
            send(slots(mine, start, size), xy_send, xy_recv.at[x, g], where)

    own_tile.wait()

    def swap_ups():
        copy(my_up, pair_up.at[y_hi], pair_send, pair_recv, place(x, (y + 2) % NY, z, core))

    def send_ups(others, recv_sem):
        own_up.wait()
        wait(pair_up.at[1 - y_hi], pair_recv)
        for where in others:
            copy(pair_up, ups.at[slot], up_send, recv_sem, where)

    early_ups, late_ups = ups.at[pl.ds(0, HALF)], ups.at[pl.ds(HALF, HALF)]

    @pl.when(first)
    def _():
        pl.semaphore_wait(barrier, CUBE - 1 + len(PLANE) + 1)
        others = [column((z + k) % CUBE) for k in range(1, CUBE)]
        for where in others:
            send(tiles.at[mine, slot], z_send, z_recv.at[0], where)
        swap_ups()
        send_ups(others, up_recv)
        ups[slot] = pair_up[...]
        wait(slots(mine, 0, CUBE - 1), z_recv.at[0])
        over_plane(0, 0, CUBE)
        pl.semaphore_wait(here, 1)
        send(slots(mine, 0, CUBE), forward_send, z_recv.at[0], column(z + CUBE))
        wait(slots(mine, CUBE, CUBE), z_recv.at[1])
        over_plane(1, CUBE, CUBE)
        wait(slots(mine, HALF, CUBE), z_recv.at[2])
        over_plane(2, HALF, CUBE)
        send(slots(mine, 0, HALF), forward_send, z_recv.at[0], column(z + 3 * CUBE))
        wait(slots(mine, 3 * CUBE, CUBE), z_recv.at[3])
        over_plane(3, 3 * CUBE, CUBE)
        wait(ups.at[pl.ds(0, HALF - 1)], up_recv)
        for k in (CUBE, 3 * CUBE):
            send(early_ups, up_forward_send, up_recv, column(z + k))

    @pl.when(second)
    def _():
        pl.semaphore_wait(barrier, HALF - 1 + len(PLANE) + 1)
        pl.semaphore_signal(here, inc=1, device_id=column(z - CUBE), device_id_type=MESH)
        for k in range(CUBE):
            send(tiles.at[mine, slot], z_send, z_recv.at[1], column(k))
        for k in range(1, CUBE):
            send(tiles.at[mine, slot], z_send, z_recv.at[1], column(CUBE + (z + k) % CUBE))
        swap_ups()
        send_ups([column(k) for k in range(CUBE)], up_recv)
        wait(slots(mine, CUBE, CUBE - 1), z_recv.at[1])
        over_plane(1, CUBE, CUBE)
        wait(slots(mine, 3 * CUBE, CUBE), z_recv.at[3])
        wait(slots(mine, 0, CUBE), z_recv.at[0])
        send(slots(mine, 0, HALF), forward_send, z_recv.at[0], column(z + CUBE))
        over_plane(0, 0, CUBE)
        over_plane(3, 3 * CUBE, CUBE)
        wait(slots(mine, HALF, CUBE), z_recv.at[2])
        over_plane(2, HALF, CUBE)
        wait(early_ups, up_recv)
        send(early_ups, up_forward_send, up_recv, column(z + CUBE))

    @pl.when(last)
    def _():
        pl.semaphore_wait(barrier, NZ - 1 + len(PLANE) + 1)
        swap_ups()
        for k in range(HALF):
            send(tiles.at[mine, slot], z_send, z_recv.at[2 + slot // (3 * CUBE)], column(k))
        for where in late_others:
            send(tiles.at[mine, slot], z_send, z_recv.at[2], where)
        send_ups([column(k) for k in range(HALF)] + late_others, up_late_recv)
        ups[slot] = pair_up[...]
        wait(slots(mine, HALF, HALF - 1), z_recv.at[2])
        over_plane(2, HALF, HALF)
        wait(slots(mine, 0, HALF), z_recv.at[0])
        over_plane(0, 0, HALF)

    def cut(a, count, start, size, which):
        return tiles.at[pl.ds(block_of(a, 0, which), count), pl.ds(start, size)]

    def arrived(a, own, g, start, size):
        wait(cut(a, NY - 1 if own else NY, start, size, core), xy_recv.at[a, g])

    columns = [((x + dx) % NX, dx == 0) for dx in (0, 1, 3, 2)]

    def arrive(a, own, lead):
        @pl.when(z < HALF)
        def _():
            for g in (0, 1) if lead else (2, 3):
                arrived(a, own, g, 0, CUBE)

        @pl.when(last)
        def _():
            arrived(a, own, 2 if lead else 0, 0, HALF)

    for a, own in columns:
        arrive(a, own, True)

    leading = jnp.where(last, HALF, 0)
    send(cut(0, NX * NY, leading, HALF, core), core_send.at[0], core_recv.at[NX], partner)

    @pl.when(z < HALF)
    def _():
        wait(late_ups, up_late_recv)

    @pl.when(last)
    def _():
        wait(early_ups, up_recv)
        wait(ups.at[pl.ds(HALF, HALF - 1)], up_late_recv)

    get_index.wait()

    iota = lambda shape, dim: lax.broadcasted_iota(jnp.int32, shape, dim)
    k32 = iota((192, 32), 0) % 64
    owner = exchanged(k32 % 16) * 2 + k32 // 32
    holds = (index[...] == owner).astype(jnp.bfloat16)
    q = iota((32, 64), 1)
    spread = (iota((32, 64), 0) == exchanged(q // 4) * 2 + (q // 2) % 2).astype(jnp.bfloat16)
    k64, q64 = iota((192, 64), 0), iota((192, 64), 1)
    pick = jnp.dot(holds, spread, preferred_element_type=jnp.float32)
    pick = jnp.where(q64 % 2 == (k64 // 16) % 2, pick, 0.0)
    pick_high = jnp.where(k64 < 128, pick, 0.0).astype(jnp.bfloat16)
    pick_low = jnp.where(k64 < 128, 0.0, pick).astype(jnp.bfloat16)
    turned = (MERGE_SCALE * ups[...].reshape(64, LANES)).T
    high = turned.astype(jnp.bfloat16)
    low = (turned - high.astype(jnp.float32)).astype(jnp.bfloat16)
    nt = (((1,), (1,)), ((), ()))
    left[...] = (lax.dot_general(high, pick_high, nt, preferred_element_type=jnp.float32)
                 + lax.dot_general(low, pick_low, nt, preferred_element_type=jnp.float32)).astype(jnp.bfloat16)
    get_weight.wait()

    def merge(a, b_low, which):
        parts = []
        for c in range(4):
            parts.append(jnp.concatenate(
                [tiles[w, :, c * 2 + i, :]
                 for w in (block_of(a, b_low, which), block_of(a, b_low + 2, which)) for i in range(2)], axis=0))
        right = jnp.concatenate(parts, axis=1)
        right_high = right.astype(jnp.bfloat16)
        right_low = (right - right_high.astype(jnp.float32)).astype(jnp.bfloat16)
        right = jnp.concatenate([right_high, right_low, right_high], axis=0)
        update = jnp.dot(left[...], right, preferred_element_type=jnp.float32)
        at = pl.ds(pl.multiple_of(((b_low * NX + a) * 2 + which) * COLUMNS, COLUMNS), COLUMNS)
        out_ref[:, at] = (weight[:, at].astype(jnp.float32) + update).astype(jnp.bfloat16)

    def from_sibling(a):
        wait(cut(a, NY, 0, HALF, 1 - core), core_recv.at[a])
        for b in range(2):
            merge(a, b, 1 - core)

    def hand_over(n):
        a, own = columns[n]
        arrive(a, own, False)
        send(cut(a, NY, HALF - leading, HALF, core), core_send.at[1], core_recv.at[a], partner)

    def merge_own(n):
        for b in range(2):
            merge(columns[n][0], b, core)

    def merge_other(n):
        if n == 0:
            wait(cut(0, NX * NY, 0, HALF, 1 - core), core_recv.at[NX])
        wait(cut(columns[n][0], NY, 0, HALF, 1 - core), core_recv.at[columns[n][0]])
        for b in range(2):
            merge(columns[n][0], b, 1 - core)

    for n in range(NX):
        hand_over(n)

    merge_own(0)
    merge_own(1)
    merge_own(2)
    merge_own(3)
    merge_other(0)
    merge_other(1)
    merge_other(2)
    merge_other(3)

    wait(pair_up.at[0], pair_send)

    @pl.when(first)
    def _():
        wait(slots(mine, 0, CUBE - 1), z_send)
        wait(ups.at[pl.ds(0, CUBE - 1)], up_send)
        wait(slots(mine, 0, 3 * CUBE), forward_send)
        wait(ups, up_forward_send)

    @pl.when(second)
    def _():
        wait(slots(mine, 0, HALF - 1), z_send)
        wait(ups.at[pl.ds(0, CUBE)], up_send)
        wait(slots(mine, 0, HALF), forward_send)
        wait(early_ups, up_forward_send)

    @pl.when(last)
    def _():
        wait(slots(mine, 0, NZ - 1), z_send)
        wait(ups.at[pl.ds(0, NZ - 1)], up_send)

    wait(tiles.at[pl.ds(0, 15)], xy_send)
    for k in range(2):
        wait(cut(0, NX * NY, 0, HALF, core), core_send.at[k])


def local(key_head_weight, down_factor_slots, adapter_up_factor, piece_slot_index):
    units, width = key_head_weight.shape[1:]
    tile = down_factor_slots.reshape(2, 4, LANES).transpose(1, 0, 2).reshape(8, LANES)
    dma = pltpu.SemaphoreType.DMA
    operands = (piece_slot_index.reshape(1, 32), tile, adapter_up_factor, key_head_weight.reshape(units, width))
    merged = pl.pallas_call(
        kernel,
        out_shape=jax.ShapeDtypeStruct((units, width), jnp.bfloat16),
        in_specs=[pl.BlockSpec(memory_space=pltpu.HBM)] * 4,
        out_specs=pl.BlockSpec(memory_space=pltpu.VMEM),
        scratch_shapes=[
            pltpu.VMEM((1, 32), jnp.int32),
            pltpu.VMEM((32, NZ, 8, LANES), jnp.float32),
            pltpu.VMEM((NZ, 2, 2, LANES), jnp.float32),
            pltpu.VMEM((2, 2, LANES), jnp.float32),
            pltpu.VMEM((units, width), jnp.bfloat16),
            pltpu.VMEM((units, 192), jnp.bfloat16),
            dma, dma((3,)), dma, dma((4,)), dma, dma, dma, dma,
            dma, pltpu.SemaphoreType.REGULAR, dma, dma, dma, dma((NX, 4)), dma((2,)), dma((NX + 1,)),
        ],
        compiler_params=pltpu.CompilerParams(
            collective_id=0, has_side_effects=True, vmem_limit_bytes=32 << 20),
        name="gather_and_merge",
    )(*[pltpu.with_memory_space_constraint(a, pltpu.HBM) for a in operands])
    return merged.reshape(1, units, width)


def solution(mesh):
    in_specs = (P("tensor", None, None), P("replica", None, "tensor"), P("replica", None), P())
    out_specs = P("tensor", None, None)
    return jax.shard_map(local, mesh=mesh, in_specs=in_specs, out_specs=out_specs, check_vma=False)
```
